32 devices in a mesh: vessel: 4 (over x, core), blk: 8 (over z, y).
Axes of the slice: x: 2, y: 2, z: 4, core: 2. Of those that a mesh axis runs over, the one named last changes fastest.
Arguments:
- populations: float32 [19, 32, 256, 128], P(None, 'vessel', 'blk'), may hold values from 0.5 to 1.5
- voxel_mask: int32 [32, 256, 128], P('vessel', 'blk'), may hold values from 0 to 2
- tracer: float32 [64, 16, 128], P('blk', 'vessel'), may hold values from -6 to 6
Outputs:
- final_populations: float32 [19, 32, 256, 128], P(None, 'vessel', 'blk')
- final_tracer: float32 [64, 16, 128], P('blk', 'vessel')
The draws below stay inside these ranges and needn't reach their ends.
All inputs are finite; a program needn't handle non-finite values.
Results may differ from the reference program's by a relative error of at most 0.0001.
Values sent between devices are 32-bit elements; how exact they have to be, the bound alone decides.
A program may use at most 128 MiB of HBM per device.

```python
import jax
import jax.numpy as jnp
import numpy as np
from jax import lax

NZ = 128
STEPS = 4
TRACER_STEPS = 2
NX = 32
NY = 256
MX = 16
MY = 128
MZ = 64


def plant(result, stream_key, smallest, largest):
    longest = result.shape.index(max(result.shape))
    spots = []
    for shift in (0, 1):
        where = [jax.random.randint(jax.random.fold_in(stream_key, axis), (), 0, length) for axis, length in enumerate(result.shape)]
        where[longest] = (where[longest] + shift) % result.shape[longest]
        spots.append(tuple(where))
    return result.at[spots[0]].set(smallest).at[spots[1]].set(largest)


def block_levels(key, dims, pieces, low, top_value):
    def one(dim, blocks):
        draws = jax.random.uniform(jax.random.fold_in(jax.random.fold_in(key, 6), dim), (blocks,), jnp.float32, low / len(pieces), top_value / len(pieces))
        return jnp.repeat(jnp.exp(draws), dims[dim] // blocks).reshape((-1,) + (1,) * (len(dims) - dim - 1))

    level = one(*pieces[0])
    for cut in pieces[1:]:
        level = level * one(*cut)
    return level


def gaussian(own_key, shape, spread, limit, pieces=(), dtype=jnp.bfloat16):
    result = spread * jax.random.normal(own_key, shape, jnp.float32)
    if pieces:
        result = result * block_levels(own_key, shape, pieces, -0.22, 0.18)
    return jnp.clip(result, -limit, limit).astype(dtype)


def setup_inputs(seed: int = 0) -> dict:
    keys = jax.random.split(jax.random.key(seed), 4)
    populations = jnp.clip(0.5 + 1.0 * jax.random.uniform(keys[0], (19, NX, NY, NZ), jnp.float32) ** block_levels(keys[0], (19, NX, NY, NZ), ((1, 4), (2, 8)), -0.2, 0.2), 0.5, 1.5)
    voxel_mask = plant(jax.random.randint(keys[1], (NX, NY, NZ), 0, 3), jax.random.fold_in(keys[1], 1), 0, 2).astype(jnp.int32)
    tracer = gaussian(keys[2], (MZ, MX, MY), 1.0, 6.0, ((0, 8), (1, 4)), jnp.float32)
    return dict(populations=populations, voxel_mask=voxel_mask, tracer=tracer)


VELOCITY = np.array([[0, 0, 0], [1, 0, 0], [-1, 0, 0], [0, 1, 0], [0, -1, 0], [0, 0, 1], [0, 0, -1], [1, 1, 0], [-1, -1, 0], [1, -1, 0], [-1, 1, 0], [1, 0, 1], [-1, 0, -1], [1, 0, -1], [-1, 0, 1], [0, 1, 1], [0, -1, -1], [0, 1, -1], [0, -1, 1]])
WEIGHTS = np.array([1.0 / 3.0] + [1.0 / 18.0] * 6 + [1.0 / 36.0] * 12)
OPPOSITE = [0, 2, 1, 4, 3, 6, 5, 8, 7, 10, 9, 12, 11, 14, 13, 16, 15, 18, 17]
relax_rate = 1.25
pore_damping = 0.5
advect_gain = 8.0
diffusion = 0.1


def moments(popul):
    weight_vec = jnp.asarray(WEIGHTS, jnp.float32)
    weight_vel = jnp.asarray(WEIGHTS[:, None] * VELOCITY, jnp.float32)
    density = jnp.einsum("i,ixyz->xyz", weight_vec, popul, precision=lax.Precision.HIGHEST)
    momentum = jnp.einsum("id,ixyz->dxyz", weight_vel, popul, precision=lax.Precision.HIGHEST)
    return density, momentum


def collide(popul, mask):
    density, momentum = moments(popul)
    velocity = momentum / density
    damped = jnp.where(mask == 1, pore_damping * velocity, velocity)
    projected = jnp.einsum("id,dxyz->ixyz", jnp.asarray(VELOCITY, jnp.float32), damped, precision=lax.Precision.HIGHEST)
    speed_sq = jnp.sum(damped * damped, axis=0)
    balance = density * (1.0 + 3.0 * projected + 4.5 * projected * projected - 1.5 * speed_sq)
    relaxed = popul + relax_rate * (balance - popul)
    bounced = jnp.stack([popul[j] for j in OPPOSITE])
    return jnp.where(mask == 2, bounced, relaxed)


def flow_velocity(popul, mask):
    density, momentum = moments(popul)
    return jnp.where(mask == 2, jnp.float32(0.0), momentum / density)


def coarsen(field):
    comps, first, second, third = field.shape
    shaped = field.reshape(comps, first // 2, 2, second // 2, 2, third // 2, 2)
    return jnp.mean(shaped, axis=(2, 4, 6))


def tracer_step(conc, flow):
    flux_x = flow[0] * conc
    flux_y = flow[1] * conc
    flux_z = flow[2] * conc
    div_x = (jnp.roll(flux_x, -1, 1) - jnp.roll(flux_x, 1, 1)) * 0.5
    div_y = (jnp.roll(flux_y, -1, 2) - jnp.roll(flux_y, 1, 2)) * 0.5
    div_z = (jnp.roll(flux_z, -1, 0) - jnp.roll(flux_z, 1, 0)) * 0.5
    divergence = div_x + div_y + div_z
    beside_all = (jnp.roll(conc, -1, 1) + jnp.roll(conc, 1, 1)) + (jnp.roll(conc, -1, 2) + jnp.roll(conc, 1, 2)) + (jnp.roll(conc, -1, 0) + jnp.roll(conc, 1, 0))
    laplace = beside_all - 6.0 * conc
    return conc - advect_gain * divergence + diffusion * laplace


def reference(populations, voxel_mask, tracer):
    state = populations
    for step in range(STEPS):
        post = collide(state, voxel_mask)
        state = jnp.stack([jnp.roll(post[i], (int(VELOCITY[i, 0]), int(VELOCITY[i, 1]), int(VELOCITY[i, 2])), axis=(0, 1, 2)) for i in range(19)])
    flow = flow_velocity(state, voxel_mask)
    coarse = jnp.transpose(coarsen(flow), (0, 3, 1, 2))
    conc = tracer
    for step in range(TRACER_STEPS):
        conc = tracer_step(conc, coarse)
    return state, conc
```

```python
import functools

import jax
import jax.numpy as jnp
import numpy as np
from jax import lax
from jax.experimental import pallas as pl
from jax.experimental.pallas import tpu as pltpu
from jax.sharding import PartitionSpec as P

STEPS = 4
TRACER_STEPS = 2

VELOCITY = [
    (0, 0, 0), (1, 0, 0), (-1, 0, 0), (0, 1, 0), (0, -1, 0), (0, 0, 1), (0, 0, -1),
    (1, 1, 0), (-1, -1, 0), (1, -1, 0), (-1, 1, 0), (1, 0, 1), (-1, 0, -1),
    (1, 0, -1), (-1, 0, 1), (0, 1, 1), (0, -1, -1), (0, 1, -1), (0, -1, 1),
]
PAIRS = [(i, i + 1) for i in range(1, 19, 2)]
ORDER = [9, 1, 11, 13, 7, 3, 15, 17, 10, 2, 12, 14, 8, 4, 16, 18, 0, 5, 6]
SLOT = {pop: k for k, pop in enumerate(ORDER)}
UP = [7, 3, 15, 17, 10]
DOWN = [8, 4, 16, 18, 9]
CORNERS = [(1, 1, 0, 0, 7), (-1, -1, 1, 0, 8), (1, -1, 1, 4, 9), (-1, 1, 0, 4, 10)]
AROUND = [(dx, dy) for dx in (-1, 0, 1) for dy in (-1, 0, 1) if (dx, dy) != (0, 0)]
MESH = pl.DeviceIdType.MESH
relax_rate = 1.25
pore_damping = 0.5
advect_gain = 8.0
diffusion = 0.1
ROW0 = 8


def moments(g):
    total = [g[i] + g[j] for i, j in PAIRS]
    diff = [g[i] - g[j] for i, j in PAIRS]
    axial = (total[0] + total[1]) + total[2]
    diagonal = ((total[3] + total[4]) + (total[5] + total[6])) + (total[7] + total[8])
    density = g[0] * (1.0 / 3.0) + axial * (1.0 / 18.0) + diagonal * (1.0 / 36.0)
    mom_x = diff[0] * (1.0 / 18.0) + ((diff[3] + diff[4]) + (diff[5] + diff[6])) * (1.0 / 36.0)
    mom_y = diff[1] * (1.0 / 18.0) + ((diff[3] - diff[4]) + (diff[7] + diff[8])) * (1.0 / 36.0)
    mom_z = diff[2] * (1.0 / 18.0) + ((diff[5] - diff[6]) + (diff[7] - diff[8])) * (1.0 / 36.0)
    return density, (mom_x, mom_y, mom_z)


def collide(g, mask):
    density, mom = moments(g)
    inverse = 1.0 / density
    factor = jnp.where(mask == 1, pore_damping * inverse, inverse)
    solid = mask == 2
    vel = [m * factor for m in mom]
    scaled = relax_rate * density
    speed_sq = vel[0] * vel[0] + vel[1] * vel[1] + vel[2] * vel[2]
    base = scaled * (1.0 - 1.5 * speed_sq)
    half = [1.5 * v for v in vel]
    linear = [(3.0 * scaled) * v for v in vel]
    keep = 1.0 - relax_rate
    post = [None] * 19
    post[0] = jnp.where(solid, g[0], base + keep * g[0])

    def along(comps, vec):
        total = None
        for c, v in zip(vec, comps):
            if c:
                part = v
                if total is None:
                    total = part if c > 0 else -part
                else:
                    total = total + part if c > 0 else total - part
        return total

    for i, j in PAIRS:
        proj = along(half, VELOCITY[i])
        odd = along(linear, VELOCITY[i])
        even = base + proj * odd
        post[i] = jnp.where(solid, g[j], (even + odd) + keep * g[i])
        post[j] = jnp.where(solid, g[i], (even - odd) + keep * g[j])
    return post


def kernel(sizes, names, pop_hbm, mask_hbm, tracer_ref, out_ref, conc_ref, pop, mask_ref, padded, ysend,
           yrecv, crecv, tracers, conc, flows, rows, coarse, gathered, load_sem, face_send, face_recv,
           tr_send, tr_recv, fl_send, fl_recv):
    vessels, blks, width, height, mz, my, reach = sizes
    tiles = height // 8
    own_rows = height // 2
    me_v = lax.axis_index(names[0])
    me_b = lax.axis_index(names[1])

    def at(dx, dy):
        return (lax.rem(me_v + dx + vessels, vessels), lax.rem(me_b + dy + blks, blks))

    last = width - 1
    spans = [(0, 1), (last, 1), (1, width - 2)]
    loads = [pltpu.make_async_copy(mask_hbm, mask_ref, load_sem.at[3])]
    for k, (start, count) in enumerate(spans):
        loads.append(
            pltpu.make_async_copy(
                pop_hbm.at[:, pl.ds(start, count)], pop.at[:, pl.ds(start, count)], load_sem.at[k]
            )
        )
    for load in loads:
        load.start()

    barrier = pltpu.get_barrier_semaphore()
    for dx in (-1, 0, 1):
        for k in range(blks):
            if dx == 0 and k == 0:
                continue
            pl.semaphore_signal(barrier, inc=1, device_id=at(dx, k), device_id_type=MESH)

    def gather(step, x, t):
        if step == 0:
            return [pop[i, x, pl.ds(8 * t, 8), :] for i in range(19)]
        g = []
        for i, (cx, cy, cz) in enumerate(VELOCITY):
            value = padded[step - 1, SLOT[i], x + 1 - cx, pl.ds(ROW0 + 8 * t - cy, 8), :]
            if cz:
                value = pltpu.roll(value, cz % 128, 1)
            g.append(value)
        return g

    def tile(step, x, t):
        g = gather(step, x, t)
        post = collide(g, mask_ref[x, pl.ds(8 * t, 8), :])
        for i in range(19):
            padded[step, SLOT[i], x + 1, pl.ds(ROW0 + 8 * t, 8), :] = post[i]
        if t == 0:
            for k, i in enumerate(DOWN):
                ysend[step, 1, k, pl.ds(x, 1), :] = post[i][0:1]
        if t == tiles - 1:
            for k, i in enumerate(UP):
                ysend[step, 0, k, pl.ds(x, 1), :] = post[i][7:8]

    def inner(step):
        def body(x, carry):
            for t in range(1, tiles - 1):
                tile(step, x, t)
            return carry

        lax.fori_loop(1, last, body, 0)

    def sides(step):
        def body(x, carry):
            tile(step, x, 0)
            tile(step, x, tiles - 1)
            return carry

        lax.fori_loop(1, last, body, 0)

    def ends(step):
        def body(k, carry):
            for t in range(tiles):
                tile(step, k * last, t)
            return carry

        lax.fori_loop(0, 2, body, 0)

    def copy(src, dst, send, recv, target):
        return pltpu.make_async_remote_copy(
            src_ref=src, dst_ref=dst, send_sem=send, recv_sem=recv, device_id=target, device_id_type=MESH
        )

    def x_copies(step):
        body = pl.ds(ROW0, height)
        found = []
        for k, (dx, first, plane, goal) in enumerate(((1, 0, width, 0), (-1, 8, 1, width + 1))):
            found.append(
                copy(
                    padded.at[step, pl.ds(first, 5), plane, body],
                    padded.at[step, pl.ds(first, 5), goal, body],
                    face_send.at[step, k], face_recv.at[step, k], at(dx, 0),
                )
            )
        return found

    def y_copies(step):
        found = []
        for k, dy in enumerate((1, -1)):
            found.append(
                copy(ysend.at[step, k], yrecv.at[step, k], face_send.at[step, 2 + k],
                     face_recv.at[step, 2 + k], at(0, dy))
            )
        for k, (dx, dy, which, place, _) in enumerate(CORNERS):
            found.append(
                copy(ysend.at[step, which, place], crecv.at[step, k], face_send.at[step, 4 + k],
                     face_recv.at[step, 4 + k], at(dx, dy))
            )
        return found

    def start(copies):
        for one in copies:
            one.start()

    def receive(step):
        beyond = ROW0 + height
        for one in y_copies(step):
            one.wait_recv()
        for x in range(width):
            for k in range(5):
                padded[step, SLOT[UP[k]], x + 1, pl.ds(ROW0 - 1, 1), :] = yrecv[step, 0, k, pl.ds(x, 1), :]
                padded[step, SLOT[DOWN[k]], x + 1, pl.ds(beyond, 1), :] = yrecv[step, 1, k, pl.ds(x, 1), :]
        for k, (dx, dy, _, _, i) in enumerate(CORNERS):
            row = ROW0 - 1 if dy == 1 else beyond
            plane, origin = (0, last) if dx == 1 else (width + 1, 0)
            padded[step, SLOT[i], plane, pl.ds(row, 1), :] = crecv[step, k, pl.ds(origin, 1), :]
        for one in x_copies(step):
            one.wait_recv()

    tr_copies = []
    for k, (dx, dy) in enumerate(AROUND):
        if dy == 0:
            src, goal = tracer_ref, pl.ds(2, mz)
        elif dy == 1:
            src, goal = tracer_ref.at[pl.ds(mz - 2, 2)], pl.ds(0, 2)
        else:
            src, goal = tracer_ref.at[pl.ds(0, 2)], pl.ds(mz + 2, 2)
        tr_copies.append(
            copy(src, tracers.at[1 - dx, goal], tr_send.at[k], tr_recv.at[k], at(dx, dy))
        )

    loads[0].wait()
    loads[1].wait()
    loads[2].wait()
    ends(0)
    pl.semaphore_wait(barrier, 3 * blks - 1)
    sent = x_copies(0)
    start(sent)
    loads[3].wait()
    sides(0)
    pending = y_copies(0)
    start(pending)
    start(tr_copies)
    sent += pending + tr_copies
    inner(0)
    tracers[1, pl.ds(2, mz)] = tracer_ref[...]
    for step in range(1, STEPS):
        inner(step)
        receive(step - 1)
        ends(step)
        pending = x_copies(step)
        start(pending)
        sent += pending
        sides(step)
        pending = y_copies(step)
        start(pending)
        sent += pending

    count = blks * reach
    line = lax.broadcasted_iota(jnp.int32, (count, 128), 0)
    cell = lax.shift_right_logical(lax.broadcasted_iota(jnp.int32, (count, 128), 1), 1)
    owner = lax.shift_right_logical(line, int(np.log2(reach)))
    offset = line - owner * reach
    wanted = owner * mz - 2 + offset
    wanted = jnp.where(wanted < 0, wanted + mz * blks, wanted)
    wanted = jnp.where(wanted >= mz * blks, wanted - mz * blks, wanted)
    spread = jnp.where((wanted == cell) & (offset < mz + 4), jnp.float32(0.125), jnp.float32(0.0))

    for one in tr_copies:
        one.wait_recv()
    conc[...] = jnp.zeros(conc.shape, jnp.float32)
    for a in range(8):
        if a < 2:
            side, cut = 0, a + 2
        elif a < 6:
            side, cut = 1, a - 2
        else:
            side, cut = 2, a - 6
        for j in range(mz + 4):
            conc[a, pl.ds(j, 1), :] = tracers[side, j, pl.ds(cut, 1), :]

    def finish(pair, t):
        sums = None
        for half in range(2):
            x = 2 * pair + half
            g = gather(STEPS, x, t)
            for i in range(19):
                out_ref[i, x, pl.ds(8 * t, 8), :] = g[i]
            density, mom = moments(g)
            inverse = jnp.where(mask_ref[x, pl.ds(8 * t, 8), :] == 2, 0.0, 1.0 / density)
            flow = [m * inverse for m in mom]
            sums = flow if sums is None else [a + b for a, b in zip(sums, flow)]
        for c in range(3):
            flows[c, pair, pl.ds(8 * t, 8), :] = sums[c]

    pairs = width // 2

    def middle(pair, carry):
        for t in range(1, tiles - 1):
            finish(pair, t)
        return carry

    def edges(pair, carry):
        finish(pair, 0)
        finish(pair, tiles - 1)
        return carry

    lax.fori_loop(1, pairs - 1, middle, 0)
    rows[...] = jnp.zeros(rows.shape, jnp.float32)
    receive(STEPS - 1)
    lax.fori_loop(1, pairs - 1, edges, 0)

    def outer(k, carry):
        for t in range(tiles):
            finish(k * (pairs - 1), t)
        return carry

    lax.fori_loop(0, 2, outer, 0)
    for p in range(2):
        for c in range(3):
            for xi in range(2):
                even = flows[c, 2 * p + xi, pl.ds(0, own_rows, 2), :]
                odd = flows[c, 2 * p + xi, pl.ds(1, own_rows, 2), :]
                rows[p, pl.ds((2 * c + xi) * own_rows, own_rows), :] = even + odd
        laid = lax.dot_general(
            spread, rows[p], (((1,), (1,)), ((), ())),
            precision=lax.Precision.HIGHEST, preferred_element_type=jnp.float32,
        )
        for b in range(blks):
            coarse[b, p] = laid[b * reach : (b + 1) * reach]

    def flow_copy(dx, goal_blk, from_blk):
        if dx == 0:
            src, dst = coarse.at[goal_blk], gathered.at[1, from_blk]
        else:
            part = 1 if dx == 1 else 0
            src, dst = coarse.at[goal_blk, part], gathered.at[1 - dx, from_blk, part]
        return copy(
            src, dst, fl_send.at[1 + dx, goal_blk], fl_recv.at[1 - dx, from_blk],
            (lax.rem(me_v + dx + vessels, vessels), goal_blk),
        )

    for k in range(blks):
        for dx in (1, -1, 0):
            if dx == 0 and k == 0:
                continue
            one = flow_copy(dx, lax.rem(me_b + k, blks), me_b)
            one.start()
            sent.append(one)
    gathered[1, me_b] = coarse[me_b]
    for one in sent:
        one.wait_send()
    for k in range(blks):
        for dx in (1, -1, 0):
            if dx == 0 and k == 0:
                continue
            flow_copy(dx, me_b, lax.rem(me_b + k, blks)).wait_recv()

    group = lax.shift_right_logical(lax.broadcasted_iota(jnp.int32, (reach, 128), 1), 4)
    flow = [[None] * 8 for _ in range(3)]
    for pair in range(4):
        side, part = ((0, 1), (1, 0), (1, 1), (2, 0))[pair]
        for c in range(3):
            for xi in range(2):
                place = 2 * c + xi
                lanes = []
                for tile_at in range(my // 128):
                    total = None
                    for b in range(8):
                        piece = gathered[side, tile_at * 8 + b, part]
                        shift = ((b - place) * 16) % 128
                        if shift:
                            piece = pltpu.roll(piece, shift, 1)
                        total = piece if total is None else jnp.where(group == b, piece, total)
                    lanes.append(total)
                flow[c][2 * pair + xi] = lanes[0] if len(lanes) == 1 else jnp.concatenate(lanes, axis=1)

    now = [conc[a] for a in range(8)]
    for step in range(TRACER_STEPS):
        new = list(now)
        for a in range(1 + step, 7 - step):
            here = now[a]
            flux_y = flow[1][a] * here
            flux_z = flow[2][a] * here
            div = (
                (flow[0][a + 1] * now[a + 1] - flow[0][a - 1] * now[a - 1])
                + (pltpu.roll(flux_y, my - 1, 1) - pltpu.roll(flux_y, 1, 1))
                + (pltpu.roll(flux_z, reach - 1, 0) - pltpu.roll(flux_z, 1, 0))
            ) * 0.5
            beside = (
                (now[a + 1] + now[a - 1])
                + (pltpu.roll(here, my - 1, 1) + pltpu.roll(here, 1, 1))
                + (pltpu.roll(here, reach - 1, 0) + pltpu.roll(here, 1, 0))
            )
            new[a] = here - advect_gain * div + diffusion * (beside - 6.0 * here)
        now = new
    for a in range(4):
        for j in range(mz):
            conc_ref[j, pl.ds(a, 1), :] = now[a + 2][j + 2 : j + 3]


def solution(mesh):
    names = ("vessel", "blk")
    vessels, blks = mesh.shape["vessel"], mesh.shape["blk"]

    def local(populations, voxel_mask, tracer):
        _, width, height, _ = populations.shape
        mz, mx, my = tracer.shape
        reach = 8 * (-(-(mz + 4) // 8))
        sizes = (vessels, blks, width, height, mz, my, reach)
        vmem = pl.BlockSpec(memory_space=pltpu.VMEM)
        hbm = pl.BlockSpec(memory_space=pl.ANY)
        f32 = jnp.float32
        dma = pltpu.SemaphoreType.DMA
        return pl.pallas_call(
            functools.partial(kernel, sizes, names),
            out_shape=(
                jax.ShapeDtypeStruct(populations.shape, f32),
                jax.ShapeDtypeStruct(tracer.shape, f32),
            ),
            in_specs=[hbm, hbm, vmem],
            out_specs=(vmem, vmem),
            scratch_shapes=[
                pltpu.VMEM(populations.shape, f32),
                pltpu.VMEM(voxel_mask.shape, jnp.int32),
                pltpu.VMEM((STEPS, 19, width + 2, height + 16, 128), f32),
                pltpu.VMEM((STEPS, 2, 5, width, 128), f32),
                pltpu.VMEM((STEPS, 2, 5, width, 128), f32),
                pltpu.VMEM((STEPS, 4, width, 128), f32),
                pltpu.VMEM((3, mz + 4, mx, my), f32),
                pltpu.VMEM((8, reach, my), f32),
                pltpu.VMEM((3, width // 2, height, 128), f32),
                pltpu.VMEM((2, 128, 128), f32),
                pltpu.VMEM((blks, 2, reach, 128), f32),
                pltpu.VMEM((3, blks, 2, reach, 128), f32),
                dma((4,)),
                dma((STEPS, 8)),
                dma((STEPS, 8)),
                dma((8,)),
                dma((8,)),
                dma((3, blks)),
                dma((3, blks)),
            ],
            compiler_params=pltpu.CompilerParams(
                collective_id=0, has_side_effects=True, vmem_limit_bytes=48 * 1024 * 1024
            ),
        )(populations, voxel_mask, tracer)

    return jax.shard_map(
        local,
        mesh=mesh,
        in_specs=(P(None, "vessel", "blk", None), P("vessel", "blk", None), P("blk", "vessel", None)),
        out_specs=(P(None, "vessel", "blk", None), P("blk", "vessel", None)),
        check_vma=False,
    )
```

```python
import functools

import jax
import jax.numpy as jnp
import numpy as np
from jax import lax
from jax.experimental import pallas as pl
from jax.experimental.pallas import tpu as pltpu
from jax.sharding import PartitionSpec as P

STEPS = 4
TRACER_STEPS = 2

VELOCITY = [
    (0, 0, 0), (1, 0, 0), (-1, 0, 0), (0, 1, 0), (0, -1, 0), (0, 0, 1), (0, 0, -1),
    (1, 1, 0), (-1, -1, 0), (1, -1, 0), (-1, 1, 0), (1, 0, 1), (-1, 0, -1),
    (1, 0, -1), (-1, 0, 1), (0, 1, 1), (0, -1, -1), (0, 1, -1), (0, -1, 1),
]
PAIRS = [(i, i + 1) for i in range(1, 19, 2)]
ORDER = [9, 1, 11, 13, 7, 3, 15, 17, 10, 2, 12, 14, 8, 4, 16, 18, 0, 5, 6]
SLOT = {pop: k for k, pop in enumerate(ORDER)}
UP = [7, 3, 15, 17, 10]
DOWN = [8, 4, 16, 18, 9]
CORNERS = [(1, 1, 0, 0, 7), (-1, -1, 1, 0, 8), (1, -1, 1, 4, 9), (-1, 1, 0, 4, 10)]
AROUND = [(dx, dy) for dx in (-1, 0, 1) for dy in (-1, 0, 1) if (dx, dy) != (0, 0)]
MESH = pl.DeviceIdType.MESH
relax_rate = 1.25
pore_damping = 0.5
advect_gain = 8.0
diffusion = 0.1
ROW0 = 8


def moments(g):
    total = [g[i] + g[j] for i, j in PAIRS]
    diff = [g[i] - g[j] for i, j in PAIRS]
    axial = (total[0] + total[1]) + total[2]
    diagonal = ((total[3] + total[4]) + (total[5] + total[6])) + (total[7] + total[8])
    density = g[0] * (1.0 / 3.0) + axial * (1.0 / 18.0) + diagonal * (1.0 / 36.0)
    mom_x = diff[0] * (1.0 / 18.0) + ((diff[3] + diff[4]) + (diff[5] + diff[6])) * (1.0 / 36.0)
    mom_y = diff[1] * (1.0 / 18.0) + ((diff[3] - diff[4]) + (diff[7] + diff[8])) * (1.0 / 36.0)
    mom_z = diff[2] * (1.0 / 18.0) + ((diff[5] - diff[6]) + (diff[7] - diff[8])) * (1.0 / 36.0)
    return density, (mom_x, mom_y, mom_z)


def collide(g, mask):
    density, mom = moments(g)
    inverse = 1.0 / density
    factor = jnp.where(mask == 1, pore_damping * inverse, inverse)
    solid = mask == 2
    vel = [m * factor for m in mom]
    scaled = relax_rate * density
    speed_sq = vel[0] * vel[0] + vel[1] * vel[1] + vel[2] * vel[2]
    base = scaled * (1.0 - 1.5 * speed_sq)
    half = [1.5 * v for v in vel]
    linear = [(3.0 * scaled) * v for v in vel]
    keep = 1.0 - relax_rate
    post = [None] * 19
    post[0] = jnp.where(solid, g[0], base + keep * g[0])

    def along(comps, vec):
        total = None
        for c, v in zip(vec, comps):
            if c:
                part = v
                if total is None:
                    total = part if c > 0 else -part
                else:
                    total = total + part if c > 0 else total - part
        return total

    for i, j in PAIRS:
        proj = along(half, VELOCITY[i])
        odd = along(linear, VELOCITY[i])
        even = base + proj * odd
        post[i] = jnp.where(solid, g[j], (even + odd) + keep * g[i])
        post[j] = jnp.where(solid, g[i], (even - odd) + keep * g[j])
    return post


def kernel(sizes, names, pop_hbm, mask_hbm, tracer_hbm, out_ref, conc_ref, pop, mask_ref, padded, ysend,
           yrecv, crecv, tracers, conc, flows, rows, coarse, gathered, load_sem, face_send, face_recv,
           tr_send, tr_recv, fl_send, fl_recv):
    vessels, blks, width, height, mz, my, reach = sizes
    tiles = height // 8
    pitch = height + 16
    own_rows = height // 2
    me_v = lax.axis_index(names[0])
    me_b = lax.axis_index(names[1])

    def at(dx, dy):
        return (lax.rem(me_v + dx + vessels, vessels), lax.rem(me_b + dy + blks, blks))

    last = width - 1
    spans = [(0, 1), (last, 1), (1, width - 2)]
    loads = [pltpu.make_async_copy(mask_hbm, mask_ref, load_sem.at[3])]
    for k, (start, count) in enumerate(spans):
        loads.append(
            pltpu.make_async_copy(
                pop_hbm.at[:, pl.ds(start, count)], pop.at[:, pl.ds(start, count)], load_sem.at[k]
            )
        )
    loads.append(pltpu.make_async_copy(tracer_hbm, tracers.at[1, pl.ds(2, mz)], load_sem.at[4]))
    for load in loads:
        load.start()

    barrier = pltpu.get_barrier_semaphore()
    for dx in (-1, 0, 1):
        for k in range(blks):
            if dx == 0 and k == 0:
                continue
            pl.semaphore_signal(barrier, inc=1, device_id=at(dx, k), device_id_type=MESH)

    def gather(step, x, t):
        if step == 0:
            return [pop[i, x, pl.ds(8 * t, 8), :] for i in range(19)]
        g = []
        for i, (cx, cy, cz) in enumerate(VELOCITY):
            value = padded[step - 1, SLOT[i], x + 1 - cx, pl.ds(ROW0 + 8 * t - cy, 8), :]
            if cz:
                value = pltpu.roll(value, cz % 128, 1)
            g.append(value)
        return g

    def tile(step, x, t):
        g = gather(step, x, t)
        post = collide(g, mask_ref[x, pl.ds(8 * t, 8), :])
        for i in range(19):
            padded[step, SLOT[i], x + 1, pl.ds(ROW0 + 8 * t, 8), :] = post[i]

    flat = padded.reshape(STEPS, 19, (width + 2) * pitch, 128)
    flat_pop = pop.reshape(19, width * height, 128)
    flat_mask = mask_ref.reshape(width * height, 128)

    def border(step):
        for which, y, names_of in ((1, 0, DOWN), (0, height - 1, UP)):
            if step == 0:
                g = [flat_pop[i, pl.ds(y, width, height), :] for i in range(19)]
            else:
                g = []
                for i, (cx, cy, cz) in enumerate(VELOCITY):
                    begin = (1 - cx) * pitch + ROW0 + y - cy
                    value = flat[step - 1, SLOT[i], pl.ds(begin, width, pitch), :]
                    if cz:
                        value = pltpu.roll(value, cz % 128, 1)
                    g.append(value)
            post = collide(g, flat_mask[pl.ds(y, width, height), :])
            for k, i in enumerate(names_of):
                ysend[step, which, k] = post[i]

    def inner(step):
        def body(x, carry):
            for t in range(1, tiles - 1):
                tile(step, x, t)
            return carry

        lax.fori_loop(1, last, body, 0)

    def sides(step):
        def body(x, carry):
            tile(step, x, 0)
            tile(step, x, tiles - 1)
            return carry

        lax.fori_loop(1, last, body, 0)

    def ends(step):
        def body(k, carry):
            for t in range(tiles):
                tile(step, k * last, t)
            return carry

        lax.fori_loop(0, 2, body, 0)

    def copy(src, dst, send, recv, target):
        return pltpu.make_async_remote_copy(
            src_ref=src, dst_ref=dst, send_sem=send, recv_sem=recv, device_id=target, device_id_type=MESH
        )

    def x_copies(step):
        body = pl.ds(ROW0, height)
        found = []
        for k, (dx, first, plane, goal) in enumerate(((1, 0, width, 0), (-1, 8, 1, width + 1))):
            found.append(
                copy(
                    padded.at[step, pl.ds(first, 5), plane, body],
                    padded.at[step, pl.ds(first, 5), goal, body],
                    face_send.at[step, k], face_recv.at[step, k], at(dx, 0),
                )
            )
        return found

    def y_copies(step):
        found = []
        for k, dy in enumerate((1, -1)):
            found.append(
                copy(ysend.at[step, k], yrecv.at[step, k], face_send.at[step, 2 + k],
                     face_recv.at[step, 2 + k], at(0, dy))
            )
        for k, (dx, dy, which, place, _) in enumerate(CORNERS):
            found.append(
                copy(ysend.at[step, which, place], crecv.at[step, k], face_send.at[step, 4 + k],
                     face_recv.at[step, 4 + k], at(dx, dy))
            )
        return found

    def start(copies):
        for one in copies:
            one.start()

    def receive(step):
        beyond = ROW0 + height
        for one in y_copies(step):
            one.wait_recv()
        for k in range(5):
            flat[step, SLOT[UP[k]], pl.ds(pitch + ROW0 - 1, width, pitch), :] = yrecv[step, 0, k]
            flat[step, SLOT[DOWN[k]], pl.ds(pitch + beyond, width, pitch), :] = yrecv[step, 1, k]
        for k, (dx, dy, _, _, i) in enumerate(CORNERS):
            row = ROW0 - 1 if dy == 1 else beyond
            plane, origin = (0, last) if dx == 1 else (width + 1, 0)
            padded[step, SLOT[i], plane, pl.ds(row, 1), :] = crecv[step, k, pl.ds(origin, 1), :]
        for one in x_copies(step):
            one.wait_recv()

    tr_copies = []
    for k, (dx, dy) in enumerate(AROUND):
        if dy == 0:
            src, goal = pl.ds(2, mz), pl.ds(2, mz)
        elif dy == 1:
            src, goal = pl.ds(mz, 2), pl.ds(0, 2)
        else:
            src, goal = pl.ds(2, 2), pl.ds(mz + 2, 2)
        tr_copies.append(
            copy(tracers.at[1, src], tracers.at[1 - dx, goal], tr_send.at[k], tr_recv.at[k], at(dx, dy))
        )

    loads[0].wait()
    loads[1].wait()
    loads[2].wait()
    ends(0)
    pl.semaphore_wait(barrier, 3 * blks - 1)
    sent = x_copies(0)
    start(sent)
    loads[3].wait()
    border(0)
    pending = y_copies(0)
    start(pending)
    sides(0)
    loads[4].wait()
    start(tr_copies)
    sent += pending + tr_copies
    inner(0)
    for step in range(1, STEPS):
        inner(step)
        receive(step - 1)
        border(step)
        pending = y_copies(step)
        start(pending)
        sent += pending
        ends(step)
        pending = x_copies(step)
        start(pending)
        sent += pending
        sides(step)

    count = blks * reach
    line = lax.broadcasted_iota(jnp.int32, (count, 128), 0)
    cell = lax.shift_right_logical(lax.broadcasted_iota(jnp.int32, (count, 128), 1), 1)
    owner = lax.shift_right_logical(line, int(np.log2(reach)))
    offset = line - owner * reach
    wanted = owner * mz - 2 + offset
    wanted = jnp.where(wanted < 0, wanted + mz * blks, wanted)
    wanted = jnp.where(wanted >= mz * blks, wanted - mz * blks, wanted)
    spread = jnp.where((wanted == cell) & (offset < mz + 4), jnp.float32(0.125), jnp.float32(0.0))

    for one in tr_copies:
        one.wait_recv()
    conc[...] = jnp.zeros(conc.shape, jnp.float32)
    for a in range(8):
        if a < 2:
            side, cut = 0, a + 2
        elif a < 6:
            side, cut = 1, a - 2
        else:
            side, cut = 2, a - 6
        for j in range(mz + 4):
            conc[a, pl.ds(j, 1), :] = tracers[side, j, pl.ds(cut, 1), :]

    def finish(pair, t):
        sums = None
        for half in range(2):
            x = 2 * pair + half
            g = gather(STEPS, x, t)
            for i in range(19):
                out_ref[i, x, pl.ds(8 * t, 8), :] = g[i]
            density, mom = moments(g)
            inverse = jnp.where(mask_ref[x, pl.ds(8 * t, 8), :] == 2, 0.0, 1.0 / density)
            flow = [m * inverse for m in mom]
            sums = flow if sums is None else [a + b for a, b in zip(sums, flow)]
        for c in range(3):
            flows[c, pair, pl.ds(8 * t, 8), :] = sums[c]

    pairs = width // 2

    def middle(pair, carry):
        for t in range(1, tiles - 1):
            finish(pair, t)
        return carry

    def edges(pair, carry):
        finish(pair, 0)
        finish(pair, tiles - 1)
        return carry

    lax.fori_loop(1, pairs - 1, middle, 0)
    rows[...] = jnp.zeros(rows.shape, jnp.float32)
    receive(STEPS - 1)
    lax.fori_loop(1, pairs - 1, edges, 0)

    def outer(k, carry):
        for t in range(tiles):
            finish(k * (pairs - 1), t)
        return carry

    lax.fori_loop(0, 2, outer, 0)
    for p in range(2):
        for c in range(3):
            for xi in range(2):
                even = flows[c, 2 * p + xi, pl.ds(0, own_rows, 2), :]
                odd = flows[c, 2 * p + xi, pl.ds(1, own_rows, 2), :]
                rows[p, pl.ds((2 * c + xi) * own_rows, own_rows), :] = even + odd
        laid = lax.dot_general(
            spread, rows[p], (((1,), (1,)), ((), ())),
            precision=lax.Precision.HIGHEST, preferred_element_type=jnp.float32,
        )
        for b in range(blks):
            coarse[b, p] = laid[b * reach : (b + 1) * reach]

    def flow_copy(dx, goal_blk, from_blk):
        if dx == 0:
            src, dst = coarse.at[goal_blk], gathered.at[1, from_blk]
        else:
            part = 1 if dx == 1 else 0
            src, dst = coarse.at[goal_blk, part], gathered.at[1 - dx, from_blk, part]
        return copy(
            src, dst, fl_send.at[1 + dx, goal_blk], fl_recv.at[1 - dx, from_blk],
            (lax.rem(me_v + dx + vessels, vessels), goal_blk),
        )

    for k in range(blks):
        for dx in (1, -1, 0):
            if dx == 0 and k == 0:
                continue
            one = flow_copy(dx, lax.rem(me_b + k, blks), me_b)
            one.start()
            sent.append(one)
    gathered[1, me_b] = coarse[me_b]
    for one in sent:
        one.wait_send()
    for k in range(blks):
        for dx in (1, -1, 0):
            if dx == 0 and k == 0:
                continue
            flow_copy(dx, me_b, lax.rem(me_b + k, blks)).wait_recv()

    group = lax.shift_right_logical(lax.broadcasted_iota(jnp.int32, (reach, 128), 1), 4)
    flow = [[None] * 8 for _ in range(3)]
    for pair in range(4):
        side, part = ((0, 1), (1, 0), (1, 1), (2, 0))[pair]
        for c in range(3):
            for xi in range(2):
                place = 2 * c + xi
                lanes = []
                for tile_at in range(my // 128):
                    total = None
                    for b in range(8):
                        piece = gathered[side, tile_at * 8 + b, part]
                        shift = ((b - place) * 16) % 128
                        if shift:
                            piece = pltpu.roll(piece, shift, 1)
                        total = piece if total is None else jnp.where(group == b, piece, total)
                    lanes.append(total)
                flow[c][2 * pair + xi] = lanes[0] if len(lanes) == 1 else jnp.concatenate(lanes, axis=1)

    now = [conc[a] for a in range(8)]
    for step in range(TRACER_STEPS):
        new = list(now)
        for a in range(1 + step, 7 - step):
            here = now[a]
            flux_y = flow[1][a] * here
            flux_z = flow[2][a] * here
            div = (
                (flow[0][a + 1] * now[a + 1] - flow[0][a - 1] * now[a - 1])
                + (pltpu.roll(flux_y, my - 1, 1) - pltpu.roll(flux_y, 1, 1))
                + (pltpu.roll(flux_z, reach - 1, 0) - pltpu.roll(flux_z, 1, 0))
            ) * 0.5
            beside = (
                (now[a + 1] + now[a - 1])
                + (pltpu.roll(here, my - 1, 1) + pltpu.roll(here, 1, 1))
                + (pltpu.roll(here, reach - 1, 0) + pltpu.roll(here, 1, 0))
            )
            new[a] = here - advect_gain * div + diffusion * (beside - 6.0 * here)
        now = new
    for a in range(4):
        for j in range(mz):
            conc_ref[j, pl.ds(a, 1), :] = now[a + 2][j + 2 : j + 3]


def solution(mesh):
    names = ("vessel", "blk")
    vessels, blks = mesh.shape["vessel"], mesh.shape["blk"]

    def local(populations, voxel_mask, tracer):
        _, width, height, _ = populations.shape
        mz, mx, my = tracer.shape
        reach = 8 * (-(-(mz + 4) // 8))
        sizes = (vessels, blks, width, height, mz, my, reach)
        vmem = pl.BlockSpec(memory_space=pltpu.VMEM)
        hbm = pl.BlockSpec(memory_space=pltpu.HBM)
        f32 = jnp.float32
        dma = pltpu.SemaphoreType.DMA
        return pl.pallas_call(
            functools.partial(kernel, sizes, names),
            out_shape=(
                jax.ShapeDtypeStruct(populations.shape, f32),
                jax.ShapeDtypeStruct(tracer.shape, f32),
            ),
            in_specs=[hbm, hbm, hbm],
            out_specs=(vmem, vmem),
            scratch_shapes=[
                pltpu.VMEM(populations.shape, f32),
                pltpu.VMEM(voxel_mask.shape, jnp.int32),
                pltpu.VMEM((STEPS, 19, width + 2, height + 16, 128), f32),
                pltpu.VMEM((STEPS, 2, 5, width, 128), f32),
                pltpu.VMEM((STEPS, 2, 5, width, 128), f32),
                pltpu.VMEM((STEPS, 4, width, 128), f32),
                pltpu.VMEM((3, mz + 4, mx, my), f32),
                pltpu.VMEM((8, reach, my), f32),
                pltpu.VMEM((3, width // 2, height, 128), f32),
                pltpu.VMEM((2, 128, 128), f32),
                pltpu.VMEM((blks, 2, reach, 128), f32),
                pltpu.VMEM((3, blks, 2, reach, 128), f32),
                dma((5,)),
                dma((STEPS, 8)),
                dma((STEPS, 8)),
                dma((8,)),
                dma((8,)),
                dma((3, blks)),
                dma((3, blks)),
            ],
            compiler_params=pltpu.CompilerParams(
                collective_id=0, has_side_effects=True, vmem_limit_bytes=54 * 1024 * 1024
            ),
        )(populations, voxel_mask, tracer)

    return jax.shard_map(
        local,
        mesh=mesh,
        in_specs=(P(None, "vessel", "blk", None), P("vessel", "blk", None), P("blk", "vessel", None)),
        out_specs=(P(None, "vessel", "blk", None), P("blk", "vessel", None)),
        check_vma=False,
    )
```

```python
import functools

import jax
import jax.numpy as jnp
import numpy as np
from jax import lax
from jax.experimental import pallas as pl
from jax.experimental.pallas import tpu as pltpu
from jax.sharding import PartitionSpec as P

STEPS = 4
TRACER_STEPS = 2

VELOCITY = [
    (0, 0, 0), (1, 0, 0), (-1, 0, 0), (0, 1, 0), (0, -1, 0), (0, 0, 1), (0, 0, -1),
    (1, 1, 0), (-1, -1, 0), (1, -1, 0), (-1, 1, 0), (1, 0, 1), (-1, 0, -1),
    (1, 0, -1), (-1, 0, 1), (0, 1, 1), (0, -1, -1), (0, 1, -1), (0, -1, 1),
]
PAIRS = [(i, i + 1) for i in range(1, 19, 2)]
ORDER = [9, 1, 11, 13, 7, 3, 15, 17, 10, 2, 12, 14, 8, 4, 16, 18, 0, 5, 6]
SLOT = {pop: k for k, pop in enumerate(ORDER)}
UP = [7, 3, 15, 17, 10]
DOWN = [8, 4, 16, 18, 9]
CORNERS = [(1, 1, 0, 0, 7), (-1, -1, 1, 0, 8), (1, -1, 1, 4, 9), (-1, 1, 0, 4, 10)]
AROUND = [(dx, dy) for dx in (-1, 0, 1) for dy in (-1, 0, 1) if (dx, dy) != (0, 0)]
MESH = pl.DeviceIdType.MESH
relax_rate = 1.25
pore_damping = 0.5
advect_gain = 8.0
diffusion = 0.1
ROW0 = 8


def moments(g):
    total = [g[i] + g[j] for i, j in PAIRS]
    diff = [g[i] - g[j] for i, j in PAIRS]
    axial = (total[0] + total[1]) + total[2]
    diagonal = ((total[3] + total[4]) + (total[5] + total[6])) + (total[7] + total[8])
    density = g[0] * (1.0 / 3.0) + axial * (1.0 / 18.0) + diagonal * (1.0 / 36.0)
    mom_x = diff[0] * (1.0 / 18.0) + ((diff[3] + diff[4]) + (diff[5] + diff[6])) * (1.0 / 36.0)
    mom_y = diff[1] * (1.0 / 18.0) + ((diff[3] - diff[4]) + (diff[7] + diff[8])) * (1.0 / 36.0)
    mom_z = diff[2] * (1.0 / 18.0) + ((diff[5] - diff[6]) + (diff[7] - diff[8])) * (1.0 / 36.0)
    return density, (mom_x, mom_y, mom_z)


def collide(g, mask):
    density, mom = moments(g)
    inverse = 1.0 / density
    factor = jnp.where(mask == 1, pore_damping * inverse, inverse)
    solid = mask == 2
    vel = [m * factor for m in mom]
    scaled = relax_rate * density
    speed_sq = vel[0] * vel[0] + vel[1] * vel[1] + vel[2] * vel[2]
    base = scaled * (1.0 - 1.5 * speed_sq)
    half = [1.5 * v for v in vel]
    linear = [(3.0 * scaled) * v for v in vel]
    keep = 1.0 - relax_rate
    post = [None] * 19
    post[0] = jnp.where(solid, g[0], base + keep * g[0])

    def along(comps, vec):
        total = None
        for c, v in zip(vec, comps):
            if c:
                part = v
                if total is None:
                    total = part if c > 0 else -part
                else:
                    total = total + part if c > 0 else total - part
        return total

    for i, j in PAIRS:
        proj = along(half, VELOCITY[i])
        odd = along(linear, VELOCITY[i])
        even = base + proj * odd
        post[i] = jnp.where(solid, g[j], (even + odd) + keep * g[i])
        post[j] = jnp.where(solid, g[i], (even - odd) + keep * g[j])
    return post


def kernel(sizes, names, pop_hbm, mask_hbm, tracer_hbm, out_ref, conc_ref, pop, mask_ref, padded, ysend,
           yrecv, crecv, tracers, conc, flows, rows, coarse, gathered, load_sem, face_send, face_recv,
           tr_send, tr_recv, fl_send, fl_recv):
    vessels, blks, width, height, mz, my, reach = sizes
    tiles = height // 8
    pitch = height + 16
    own_rows = height // 2
    me_v = lax.axis_index(names[0])
    me_b = lax.axis_index(names[1])

    def at(dx, dy):
        return (lax.rem(me_v + dx + vessels, vessels), lax.rem(me_b + dy + blks, blks))

    last = width - 1
    spans = [(0, 1), (last, 1), (1, width - 2)]
    loads = [pltpu.make_async_copy(mask_hbm, mask_ref, load_sem.at[3])]
    for k, (start, count) in enumerate(spans):
        loads.append(
            pltpu.make_async_copy(
                pop_hbm.at[:, pl.ds(start, count)], pop.at[:, pl.ds(start, count)], load_sem.at[k]
            )
        )
    loads.append(pltpu.make_async_copy(tracer_hbm, tracers.at[1, pl.ds(2, mz)], load_sem.at[4]))
    for load in loads:
        load.start()

    barrier = pltpu.get_barrier_semaphore()
    for dx in (-1, 0, 1):
        for k in range(blks):
            if dx == 0 and k == 0:
                continue
            pl.semaphore_signal(barrier, inc=1, device_id=at(dx, k), device_id_type=MESH)

    def gather(step, x, t):
        if step == 0:
            return [pop[i, x, pl.ds(8 * t, 8), :] for i in range(19)]
        g = []
        for i, (cx, cy, cz) in enumerate(VELOCITY):
            value = padded[step - 1, SLOT[i], x + 1 - cx, pl.ds(ROW0 + 8 * t - cy, 8), :]
            if cz:
                value = pltpu.roll(value, cz % 128, 1)
            g.append(value)
        return g

    def tile(step, x, t):
        g = gather(step, x, t)
        post = collide(g, mask_ref[x, pl.ds(8 * t, 8), :])
        for i in range(19):
            padded[step, SLOT[i], x + 1, pl.ds(ROW0 + 8 * t, 8), :] = post[i]

    flat = padded.reshape(STEPS, 19, (width + 2) * pitch, 128)
    flat_pop = pop.reshape(19, width * height, 128)
    flat_mask = mask_ref.reshape(width * height, 128)

    def border(step):
        for which, y, names_of in ((1, 0, DOWN), (0, height - 1, UP)):
            if step == 0:
                g = [flat_pop[i, pl.ds(y, width, height), :] for i in range(19)]
            else:
                g = []
                for i, (cx, cy, cz) in enumerate(VELOCITY):
                    begin = (1 - cx) * pitch + ROW0 + y - cy
                    value = flat[step - 1, SLOT[i], pl.ds(begin, width, pitch), :]
                    if cz:
                        value = pltpu.roll(value, cz % 128, 1)
                    g.append(value)
            post = collide(g, flat_mask[pl.ds(y, width, height), :])
            for k, i in enumerate(names_of):
                ysend[step, which, k] = post[i]

    def inner(step):
        def body(x, carry):
            for t in range(1, tiles - 1):
                tile(step, x, t)
            return carry

        lax.fori_loop(1, last, body, 0)

    def sides(step):
        def body(x, carry):
            tile(step, x, 0)
            tile(step, x, tiles - 1)
            return carry

        lax.fori_loop(1, last, body, 0)

    def ends(step):
        def body(k, carry):
            for t in range(tiles):
                tile(step, k * last, t)
            return carry

        lax.fori_loop(0, 2, body, 0)

    def copy(src, dst, send, recv, target):
        return pltpu.make_async_remote_copy(
            src_ref=src, dst_ref=dst, send_sem=send, recv_sem=recv, device_id=target, device_id_type=MESH
        )

    def x_copies(step):
        body = pl.ds(ROW0, height)
        found = []
        for k, (dx, first, plane, goal) in enumerate(((1, 0, width, 0), (-1, 8, 1, width + 1))):
            found.append(
                copy(
                    padded.at[step, pl.ds(first, 5), plane, body],
                    padded.at[step, pl.ds(first, 5), goal, body],
                    face_send.at[step, k], face_recv.at[step, k], at(dx, 0),
                )
            )
        return found

    def y_copies(step):
        found = []
        for k, dy in enumerate((1, -1)):
            found.append(
                copy(ysend.at[step, k], yrecv.at[step, k], face_send.at[step, 2 + k],
                     face_recv.at[step, 2 + k], at(0, dy))
            )
        for k, (dx, dy, which, place, _) in enumerate(CORNERS):
            found.append(
                copy(ysend.at[step, which, place], crecv.at[step, k], face_send.at[step, 4 + k],
                     face_recv.at[step, 4 + k], at(dx, dy))
            )
        return found

    def start(copies):
        for one in copies:
            one.start()

    def receive(step):
        beyond = ROW0 + height
        for one in y_copies(step):
            one.wait_recv()
        for k in range(5):
            flat[step, SLOT[UP[k]], pl.ds(pitch + ROW0 - 1, width, pitch), :] = yrecv[step, 0, k]
            flat[step, SLOT[DOWN[k]], pl.ds(pitch + beyond, width, pitch), :] = yrecv[step, 1, k]
        for k, (dx, dy, _, _, i) in enumerate(CORNERS):
            row = ROW0 - 1 if dy == 1 else beyond
            plane, origin = (0, last) if dx == 1 else (width + 1, 0)
            padded[step, SLOT[i], plane, pl.ds(row, 1), :] = crecv[step, k, pl.ds(origin, 1), :]
        for one in x_copies(step):
            one.wait_recv()

    tr_copies = []
    for k, (dx, dy) in enumerate(AROUND):
        if dy == 0:
            src, goal = pl.ds(2, mz), pl.ds(2, mz)
        elif dy == 1:
            src, goal = pl.ds(mz, 2), pl.ds(0, 2)
        else:
            src, goal = pl.ds(2, 2), pl.ds(mz + 2, 2)
        tr_copies.append(
            copy(tracers.at[1, src], tracers.at[1 - dx, goal], tr_send.at[k], tr_recv.at[k], at(dx, dy))
        )

    loads[0].wait()
    loads[1].wait()
    loads[2].wait()
    loads[3].wait()
    border(0)
    pl.semaphore_wait(barrier, 3 * blks - 1)
    pending = y_copies(0)
    start(pending)
    ends(0)
    sent = x_copies(0)
    start(sent)
    sides(0)
    loads[4].wait()
    start(tr_copies)
    sent += pending + tr_copies
    inner(0)
    for step in range(1, STEPS):
        inner(step)
        receive(step - 1)
        border(step)
        pending = y_copies(step)
        start(pending)
        sent += pending
        ends(step)
        pending = x_copies(step)
        start(pending)
        sent += pending
        sides(step)

    count = blks * reach
    line = lax.broadcasted_iota(jnp.int32, (count, 128), 0)
    cell = lax.shift_right_logical(lax.broadcasted_iota(jnp.int32, (count, 128), 1), 1)
    owner = lax.shift_right_logical(line, int(np.log2(reach)))
    offset = line - owner * reach
    wanted = owner * mz - 2 + offset
    wanted = jnp.where(wanted < 0, wanted + mz * blks, wanted)
    wanted = jnp.where(wanted >= mz * blks, wanted - mz * blks, wanted)
    spread = jnp.where((wanted == cell) & (offset < mz + 4), jnp.float32(0.125), jnp.float32(0.0))

    for one in tr_copies:
        one.wait_recv()
    conc[...] = jnp.zeros(conc.shape, jnp.float32)
    for a in range(8):
        if a < 2:
            side, cut = 0, a + 2
        elif a < 6:
            side, cut = 1, a - 2
        else:
            side, cut = 2, a - 6
        for j in range(mz + 4):
            conc[a, pl.ds(j, 1), :] = tracers[side, j, pl.ds(cut, 1), :]

    def finish(pair, t):
        sums = None
        for half in range(2):
            x = 2 * pair + half
            g = gather(STEPS, x, t)
            density, mom = moments(g)
            inverse = jnp.where(mask_ref[x, pl.ds(8 * t, 8), :] == 2, 0.0, 1.0 / density)
            flow = [m * inverse for m in mom]
            sums = flow if sums is None else [a + b for a, b in zip(sums, flow)]
        for c in range(3):
            flows[c, pair, pl.ds(8 * t, 8), :] = sums[c]

    pairs = width // 2

    def middle(pair, carry):
        for t in range(1, tiles - 1):
            finish(pair, t)
        return carry

    def edges(pair, carry):
        finish(pair, 0)
        finish(pair, tiles - 1)
        return carry

    lax.fori_loop(1, pairs - 1, middle, 0)
    rows[...] = jnp.zeros(rows.shape, jnp.float32)
    receive(STEPS - 1)
    lax.fori_loop(1, pairs - 1, edges, 0)

    def outer(k, carry):
        for t in range(tiles):
            finish(k * (pairs - 1), t)
        return carry

    lax.fori_loop(0, 2, outer, 0)
    for p in range(2):
        for c in range(3):
            for xi in range(2):
                even = flows[c, 2 * p + xi, pl.ds(0, own_rows, 2), :]
                odd = flows[c, 2 * p + xi, pl.ds(1, own_rows, 2), :]
                rows[p, pl.ds((2 * c + xi) * own_rows, own_rows), :] = even + odd
        laid = lax.dot_general(
            spread, rows[p], (((1,), (1,)), ((), ())),
            precision=lax.Precision.HIGHEST, preferred_element_type=jnp.float32,
        )
        for b in range(blks):
            coarse[b, p] = laid[b * reach : (b + 1) * reach]

    def flow_copy(dx, goal_blk, from_blk):
        if dx == 0:
            src, dst = coarse.at[goal_blk], gathered.at[1, from_blk]
        else:
            part = 1 if dx == 1 else 0
            src, dst = coarse.at[goal_blk, part], gathered.at[1 - dx, from_blk, part]
        return copy(
            src, dst, fl_send.at[1 + dx, goal_blk], fl_recv.at[1 - dx, from_blk],
            (lax.rem(me_v + dx + vessels, vessels), goal_blk),
        )

    for k in range(blks):
        for dx in (1, -1, 0):
            if dx == 0 and k == 0:
                continue
            one = flow_copy(dx, lax.rem(me_b + k, blks), me_b)
            one.start()
            sent.append(one)
    gathered[1, me_b] = coarse[me_b]

    def emit(x, carry):
        for t in range(tiles):
            g = gather(STEPS, x, t)
            for i in range(19):
                out_ref[i, x, pl.ds(8 * t, 8), :] = g[i]
        return carry

    lax.fori_loop(0, width, emit, 0)
    for one in sent:
        one.wait_send()
    for k in range(blks):
        for dx in (1, -1, 0):
            if dx == 0 and k == 0:
                continue
            flow_copy(dx, me_b, lax.rem(me_b + k, blks)).wait_recv()

    group = lax.shift_right_logical(lax.broadcasted_iota(jnp.int32, (reach, 128), 1), 4)
    flow = [[None] * 8 for _ in range(3)]
    for pair in range(4):
        side, part = ((0, 1), (1, 0), (1, 1), (2, 0))[pair]
        for c in range(3):
            for xi in range(2):
                place = 2 * c + xi
                lanes = []
                for tile_at in range(my // 128):
                    total = None
                    for b in range(8):
                        piece = gathered[side, tile_at * 8 + b, part]
                        shift = ((b - place) * 16) % 128
                        if shift:
                            piece = pltpu.roll(piece, shift, 1)
                        total = piece if total is None else jnp.where(group == b, piece, total)
                    lanes.append(total)
                flow[c][2 * pair + xi] = lanes[0] if len(lanes) == 1 else jnp.concatenate(lanes, axis=1)

    now = [conc[a] for a in range(8)]
    for step in range(TRACER_STEPS):
        new = list(now)
        for a in range(1 + step, 7 - step):
            here = now[a]
            flux_y = flow[1][a] * here
            flux_z = flow[2][a] * here
            div = (
                (flow[0][a + 1] * now[a + 1] - flow[0][a - 1] * now[a - 1])
                + (pltpu.roll(flux_y, my - 1, 1) - pltpu.roll(flux_y, 1, 1))
                + (pltpu.roll(flux_z, reach - 1, 0) - pltpu.roll(flux_z, 1, 0))
            ) * 0.5
            beside = (
                (now[a + 1] + now[a - 1])
                + (pltpu.roll(here, my - 1, 1) + pltpu.roll(here, 1, 1))
                + (pltpu.roll(here, reach - 1, 0) + pltpu.roll(here, 1, 0))
            )
            new[a] = here - advect_gain * div + diffusion * (beside - 6.0 * here)
        now = new
    for a in range(4):
        for j in range(mz):
            conc_ref[j, pl.ds(a, 1), :] = now[a + 2][j + 2 : j + 3]


def solution(mesh):
    names = ("vessel", "blk")
    vessels, blks = mesh.shape["vessel"], mesh.shape["blk"]

    def local(populations, voxel_mask, tracer):
        _, width, height, _ = populations.shape
        mz, mx, my = tracer.shape
        reach = 8 * (-(-(mz + 4) // 8))
        sizes = (vessels, blks, width, height, mz, my, reach)
        vmem = pl.BlockSpec(memory_space=pltpu.VMEM)
        hbm = pl.BlockSpec(memory_space=pltpu.HBM)
        f32 = jnp.float32
        dma = pltpu.SemaphoreType.DMA
        return pl.pallas_call(
            functools.partial(kernel, sizes, names),
            out_shape=(
                jax.ShapeDtypeStruct(populations.shape, f32),
                jax.ShapeDtypeStruct(tracer.shape, f32),
            ),
            in_specs=[hbm, hbm, hbm],
            out_specs=(vmem, vmem),
            scratch_shapes=[
                pltpu.VMEM(populations.shape, f32),
                pltpu.VMEM(voxel_mask.shape, jnp.int32),
                pltpu.VMEM((STEPS, 19, width + 2, height + 16, 128), f32),
                pltpu.VMEM((STEPS, 2, 5, width, 128), f32),
                pltpu.VMEM((STEPS, 2, 5, width, 128), f32),
                pltpu.VMEM((STEPS, 4, width, 128), f32),
                pltpu.VMEM((3, mz + 4, mx, my), f32),
                pltpu.VMEM((8, reach, my), f32),
                pltpu.VMEM((3, width // 2, height, 128), f32),
                pltpu.VMEM((2, 128, 128), f32),
                pltpu.VMEM((blks, 2, reach, 128), f32),
                pltpu.VMEM((3, blks, 2, reach, 128), f32),
                dma((5,)),
                dma((STEPS, 8)),
                dma((STEPS, 8)),
                dma((8,)),
                dma((8,)),
                dma((3, blks)),
                dma((3, blks)),
            ],
            compiler_params=pltpu.CompilerParams(
                collective_id=0, has_side_effects=True, vmem_limit_bytes=51 * 1024 * 1024
            ),
        )(populations, voxel_mask, tracer)

    return jax.shard_map(
        local,
        mesh=mesh,
        in_specs=(P(None, "vessel", "blk", None), P("vessel", "blk", None), P("blk", "vessel", None)),
        out_specs=(P(None, "vessel", "blk", None), P("blk", "vessel", None)),
        check_vma=False,
    )
```
